32 devices in a mesh: child: 2 (over core), row: 4 (over y, x), col: 4 (over z).
Axes of the slice: x: 2, y: 2, z: 4, core: 2. Of those that a mesh axis runs over, the one named last changes fastest.
Arguments:
- schur_blocks: bfloat16 [2, 16384, 16384], P('child', 'row', 'col'), may hold values from -2 to 2
- child_map: int32 [2, 16384], replicated, may hold values from 0 to 24575, as said below
- round_seeds: int32 [2], replicated, may hold values from 1 to 999999
Outputs:
- leaf_bases: float32 [24576, 256], P(('row', 'child', 'col'))
- fresh_samples: float32 [24576, 256], P(('row', 'child', 'col'))
The draws below stay inside these ranges and needn't reach their ends.
Inputs may be any that keep to these rules, and one draw needn't show every extreme that they name: For each child c and each block r < 4, the entries child_map[c, r * 4096 : (r + 1) * 4096] rise strictly, lie in parent rows [r * 6144, (r + 1) * 6144), and include both ends of that range.
All inputs are finite; a program needn't handle non-finite values.
Results may differ from the reference program's by a relative error of at most 0.0031.
Values sent between devices are 32-bit elements; how exact they have to be, the bound alone decides.
No kernel may reach another device: no remote copies, remote signals or barrier semaphores. Data moves between devices by JAX's collectives and lax.ppermute only.
A program may use at most 128 MiB of HBM per device.

```python
import math
import jax
import jax.numpy as jnp
from jax import lax

NC = 16384
NP = 24576
K = 256
NCB = 4096
NPB = 6144


def draw_schur_blocks(key, part):
    key_main = jax.random.fold_in(key, 101)
    key_base, key_scale = jax.random.split(key_main)
    base_draw = jnp.clip(jax.random.normal(key_base, (2, NC, NC), jnp.float32), -4.0, 4.0)
    spread = jax.random.uniform(key_scale, (2, NC), jnp.float32, 0.0, math.log(10.0 / 3.0))
    within = (jnp.arange(NC) % NCB).astype(jnp.float32) / NCB
    row_scale = jnp.exp(within * math.log(3.0))[None, :] * jnp.exp(spread)
    return (base_draw * row_scale[:, :, None] * NC ** (-0.5)).astype(jnp.bfloat16)


def one_block_map(block_key, block_number):
    interior = jax.random.permutation(block_key, NPB - 2)[:NCB - 2] + 1
    chosen = jnp.concatenate([jnp.zeros((1,), jnp.int32), interior.astype(jnp.int32), jnp.full((1,), NPB - 1, jnp.int32)])
    return jnp.sort(chosen) + block_number * NPB


def draw_child_map(key, part):
    key_main = jax.random.fold_in(key, 23)
    block_total = NC // NCB
    block_keys = jax.random.split(key_main, 2 * block_total)
    block_numbers = jnp.tile(jnp.arange(block_total, dtype=jnp.int32), 2)
    mapped = jax.vmap(one_block_map)(block_keys, block_numbers)
    return mapped.reshape(2, NC).astype(jnp.int32)


def setup_inputs(seed: int = 0) -> dict:
    splits = jax.random.split(jax.random.key(seed), 4)
    schur_blocks = draw_schur_blocks(jax.random.fold_in(splits[3], 71), 0)
    child_map = draw_child_map(jax.random.fold_in(splits[3], 71), 0)
    round_seeds = jax.random.randint(splits[2], (2,), 1, 1000000).astype(jnp.int32)
    return dict(schur_blocks=schur_blocks, child_map=child_map, round_seeds=round_seeds)


def sample_rows(seed_value, parents, sample_width):
    hashed = parents[:, None] * 40503 + lax.iota(jnp.int32, sample_width)[None, :] * 9973 + seed_value * 2654435
    hashed = hashed ^ hashed >> 15 & 131071
    hashed = hashed * 73244475
    hashed = hashed ^ hashed >> 13 & 524287
    hashed = hashed * 1274126177
    hashed = hashed ^ hashed >> 16 & 65535
    unit_value = (hashed & 16777215).astype(jnp.float32) * (1.0 / 16777216.0)
    return (unit_value - 0.5) * 3.4641016

def project_leaf(first_leaf, second_leaf):
    gram_matrix = jnp.dot(first_leaf.T, first_leaf, precision=lax.Precision.HIGHEST) / NPB
    lower_factor = jnp.linalg.cholesky(gram_matrix)
    leaf_basis = lax.linalg.triangular_solve(lower_factor, first_leaf, left_side=False, lower=True, transpose_a=True)
    coefficients = jnp.dot(leaf_basis.T, second_leaf, precision=lax.Precision.HIGHEST) / NPB
    return (leaf_basis, second_leaf - jnp.dot(leaf_basis, coefficients, precision=lax.Precision.HIGHEST))

def reference(schur_blocks, child_map, round_seeds):
    parents = jnp.arange(NP, dtype=jnp.int32)
    samples = jnp.concatenate([sample_rows(round_seeds[0], parents, K), sample_rows(round_seeds[1], parents, K)], axis=1).astype(jnp.bfloat16)
    parent_sketch = jnp.zeros((NP, 2 * K), jnp.float32)
    for child_number in range(2):
        mapped = child_map[child_number]
        child_sketch = jnp.dot(schur_blocks[child_number].astype(jnp.float32), samples[mapped].astype(jnp.float32), preferred_element_type=jnp.float32)
        parent_sketch = parent_sketch.at[mapped].add(child_sketch)
    leaves = parent_sketch.reshape(NP // NPB, NPB, 2 * K)
    leaf_bases, fresh_samples = jax.vmap(project_leaf)(leaves[:, :, :K], leaves[:, :, K:])
    return (leaf_bases.reshape(NP, K), fresh_samples.reshape(NP, K))
```

```python
import functools

import jax
import jax.numpy as jnp
import numpy as np
from jax import lax
from jax.experimental import pallas as pl
from jax.experimental.pallas import tpu as pltpu
from jax.sharding import PartitionSpec as P

NP = 24576
K = 256
HI = lax.Precision.HIGHEST
CORES = [(0, 1), (1, 0)]
MIB = 1024 * 1024


def sample_rows(seed_value, parents, sample_width):
    hashed = (
        parents[:, None] * 40503
        + lax.iota(jnp.int32, sample_width)[None, :] * 9973
        + seed_value * 2654435
    )
    hashed = hashed ^ hashed >> 15 & 131071
    hashed = hashed * 73244475
    hashed = hashed ^ hashed >> 13 & 524287
    hashed = hashed * 1274126177
    hashed = hashed ^ hashed >> 16 & 65535
    unit_value = (hashed & 16777215).astype(jnp.float32) * (1.0 / 16777216.0)
    return (unit_value - 0.5) * 3.4641016


def block_sizes(own_rows, block_rows):
    piece = own_rows // 2 if own_rows % 32 == 0 and own_rows >= 256 else own_rows
    window = min(piece + 16, block_rows)
    tile = max(d for d in range(8, min(piece, 240) + 1, 8) if piece % d == 0)
    reach = min(256, window)
    return piece, window, tile, reach


def block_kernel(sizes, steps, scal_ref, ids_ref, schur_ref, samples_ref, *rest):
    piece, window, tile, reach = sizes
    mine_ref, other_ref, held, total, sems = rest[-5:]
    depth = held.shape[0]
    step = pl.program_id(0)

    def copy(s):
        slot = lax.rem(s, depth)
        first = pl.multiple_of(scal_ref[s, 0], 16)
        return pltpu.make_async_copy(schur_ref.at[pl.ds(first, window), :], held.at[slot], sems.at[slot])

    @pl.when(step == 0)
    def _():
        for s in range(min(depth - 1, steps)):
            copy(s).start()

    @pl.when(step + depth - 1 < steps)
    def _():
        copy(step + depth - 1).start()

    copy(step).wait()
    total[...] = jnp.dot(
        held[lax.rem(step, depth)], samples_ref[...], preferred_element_type=jnp.float32
    )

    def spread(out_ref):
        for i in range(piece // tile):
            first = pl.multiple_of(scal_ref[step, 2 + i], 16)
            child = scal_ref[step, 0] + first
            lane = pl.multiple_of(child // 128 * 128, 128)
            ids = pltpu.roll(ids_ref[:, pl.ds(lane, 384)], lax.rem(384 - (child - lane), 384), 1)
            ids = jnp.broadcast_to(ids[0:1, :reach], (tile, reach))
            wanted = scal_ref[step, 1] + i * tile + lax.broadcasted_iota(jnp.int32, (tile, reach), 0)
            select = (ids == wanted).astype(jnp.float32).astype(jnp.bfloat16)
            values = total[pl.ds(first, reach), :]
            high = values.astype(jnp.bfloat16)
            low = (values - high.astype(jnp.float32)).astype(jnp.bfloat16)
            out_ref[i * tile : (i + 1) * tile, :] = jnp.dot(
                select, high, preferred_element_type=jnp.float32
            ) + jnp.dot(select, low, preferred_element_type=jnp.float32)

    @pl.when(lax.rem(step, 2) == 0)
    def _():
        spread(other_ref)

    @pl.when(lax.rem(step, 2) == 1)
    def _():
        spread(mine_ref)


def block_scalars(row_ids, bases, own_rows, sizes):
    piece, window, tile, reach = sizes
    block_rows = row_ids.shape[0]
    bases = (bases.reshape(-1, 1, 2)[:, :, ::-1] + lax.iota(jnp.int32, own_rows // piece)[None, :, None] * piece).reshape(-1)
    starts = bases[:, None] + lax.iota(jnp.int32, piece // tile)[None, :] * tile
    before = jnp.sum((row_ids[None, None, :] < starts[:, :, None]).astype(jnp.int32), axis=2)
    first = jnp.minimum(before[:, :1] // 16 * 16, block_rows - window)
    inner = jnp.minimum((before - first) // 16 * 16, window - reach)
    return jnp.concatenate([first, bases[:, None], inner], axis=1)


def sketch_pair(scalars, ids, child_block, samples, own_rows, sizes, after=()):
    piece, window, _, _ = sizes
    steps = scalars.shape[0]
    block_cols = child_block.shape[1]
    width = samples.shape[1]
    grid_spec = pltpu.PrefetchScalarGridSpec(
        num_scalar_prefetch=1,
        grid=(steps,),
        in_specs=[
            pl.BlockSpec(memory_space=pltpu.VMEM),
            pl.BlockSpec(memory_space=pl.ANY),
            pl.BlockSpec(memory_space=pltpu.VMEM),
        ]
        + [pl.BlockSpec(memory_space=pl.ANY)] * len(after),
        out_specs=[pl.BlockSpec((piece, width), lambda s, _: (s // 2, 0))] * 2,
        scratch_shapes=[
            pltpu.VMEM((3, window, block_cols), jnp.bfloat16),
            pltpu.VMEM((window, width), jnp.float32),
            pltpu.SemaphoreType.DMA((3,)),
        ],
    )
    return pl.pallas_call(
        functools.partial(block_kernel, sizes, steps),
        out_shape=[jax.ShapeDtypeStruct((own_rows, width), jnp.float32)] * 2,
        grid_spec=grid_spec,
        compiler_params=pltpu.CompilerParams(vmem_limit_bytes=24 * MIB),
        cost_estimate=pl.CostEstimate(
            flops=2 * steps * window * block_cols * width,
            bytes_accessed=2 * steps * window * block_cols,
            transcendentals=0,
        ),
        name="sketch",
    )(scalars, ids, child_block, samples, *after)


def eliminate(tiles, size):
    count = size // 8
    sub = lax.broadcasted_iota(jnp.int32, (8, size), 0)
    lane = lax.broadcasted_iota(jnp.int32, (8, size), 1)
    rows = list(tiles)
    inverse = [(lane == sub + 8 * t).astype(jnp.float32) for t in range(count)]

    def row(value, k):
        return jnp.broadcast_to(value[k : k + 1, :], (8, size))

    for t in range(count):
        columns = [
            [jnp.broadcast_to(rows[i][:, 8 * t + k : 8 * t + k + 1], (8, size)) for k in range(8)]
            for i in range(t, count)
        ]
        diagonal = jnp.ones((8, size), jnp.float32)
        for k in range(8):
            pivot = row(columns[0][k], k)
            scale = 1.0 / pivot
            diagonal = jnp.where(sub == k, pivot, diagonal)
            heads = [row(columns[0][l], k) * scale for l in range(k + 1, 8)]
            head_row = row(rows[t], k) * scale
            head_inv = row(inverse[t], k) * scale
            for i in range(t, count):
                factor = columns[i - t][k]
                if i == t:
                    factor = jnp.where(sub > k, factor, 0.0)
                for l in range(k + 1, 8):
                    columns[i - t][l] = columns[i - t][l] - factor * heads[l - k - 1]
                rows[i] = rows[i] - factor * head_row
                inverse[i] = inverse[i] - factor * head_inv
        inverse[t] = inverse[t] * lax.rsqrt(diagonal)
    return jnp.concatenate(inverse, axis=0)


def factor_kernel(gram_ref, out_ref):
    half = gram_ref.shape[0] // 2

    def dot(a, b, dims):
        return lax.dot_general(a, b, (dims, ((), ())), precision=HI, preferred_element_type=jnp.float32)

    first = eliminate([gram_ref[8 * t : 8 * t + 8, :half] for t in range(half // 8)], half)
    lower = dot(gram_ref[half:, :half], first, ((1,), (1,)))
    rest = gram_ref[half:, half:] - dot(lower, lower, ((1,), (1,)))
    second = eliminate([rest[8 * t : 8 * t + 8, :] for t in range(half // 8)], half)
    out_ref[:half, :half] = first
    out_ref[:half, half:] = jnp.zeros((half, half), jnp.float32)
    out_ref[half:, :half] = -dot(second, dot(lower, first, ((1,), (0,))), ((1,), (0,)))
    out_ref[half:, half:] = second


def inverse_factor(gram):
    return pl.pallas_call(
        factor_kernel,
        out_shape=jax.ShapeDtypeStruct(gram.shape, jnp.float32),
        compiler_params=pltpu.CompilerParams(vmem_limit_bytes=16 * MIB),
        name="inverse_factor",
    )(gram)


ORDER = np.array([[3, 2, 1, 0], [3, 2, 0, 1], [0, 1, 3, 2], [0, 1, 2, 3]], np.int32)
INWARD = [(0, 1), (3, 2)]
ACROSS = [(1, 2), (2, 1)]
PAIRS = [(0, 1), (1, 0), (2, 3), (3, 2)]


def hop(value, pairs):
    return lax.ppermute(value, "col", pairs)


def line_scatter(make, after):
    own0 = make(0, after[0])
    in3 = [hop(own, INWARD) for own in own0]
    own1 = make(1, after[1] if 1 in after else own0[:1])
    mid1 = [hop(own + step, ACROSS) for own, step in zip(own0, in3)]
    in2 = [hop(own, INWARD) for own in own1]
    own2 = make(2, mid1[:1])
    mid2 = [hop(own + step, ACROSS) for own, step in zip(own1, in2)]
    own3 = make(3, mid1[1:])
    last = [hop(own + step, PAIRS) for own, step in zip(own2, mid1)]
    return [sum(terms) for terms in zip(own3, mid2, last)], [mid2[0], last[0]]


def line_sum(value):
    value = value + hop(value, PAIRS)
    return value + hop(value, [(0, 2), (2, 0), (1, 3), (3, 1)])


def group_sum(value, child_index):
    half = value.shape[0] // 2
    mine = lax.dynamic_slice_in_dim(value, child_index * half, half)
    other = lax.dynamic_slice_in_dim(value, (1 - child_index) * half, half)
    mine = line_sum(mine + lax.ppermute(other, "child", CORES))
    other = lax.ppermute(mine, "child", CORES)
    low = jnp.where(child_index == 0, mine, other)
    high = jnp.where(child_index == 0, other, mine)
    return jnp.concatenate([low, high], axis=0)


def body(schur_blocks, child_map, round_seeds):
    child_block = schur_blocks[0]
    block_rows, block_cols = child_block.shape
    child_count = lax.axis_size("child")
    col_count = lax.axis_size("col")
    row_count = lax.axis_size("row")
    child_index = lax.axis_index("child")
    row_index = lax.axis_index("row")
    col_index = lax.axis_index("col")
    own_map = lax.dynamic_index_in_dim(child_map, child_index, 0, keepdims=False)
    col_ids = lax.dynamic_slice_in_dim(own_map, col_index * block_cols, block_cols)
    row_ids = lax.dynamic_slice_in_dim(own_map, row_index * block_rows, block_rows)
    leaf_rows = NP // row_count
    own_rows = leaf_rows // (child_count * col_count)
    leaf_base = row_index * leaf_rows
    sizes = block_sizes(own_rows, block_rows)
    ids = jnp.broadcast_to(jnp.pad(row_ids, (0, 384), constant_values=-1)[None, :], (8, block_rows + 384))
    samples = [
        sample_rows(round_seeds[r], col_ids, K).astype(jnp.bfloat16) for r in range(round_seeds.shape[0])
    ]

    if child_count == 2 and col_count == len(ORDER):
        places = lax.dynamic_index_in_dim(jnp.asarray(ORDER), col_index, 0, keepdims=False)
        halves = jnp.stack([child_index, 1 - child_index])
        bases = leaf_base + (halves[None, :] * col_count + places[:, None]) * own_rows
        scalars = block_scalars(row_ids, bases.reshape(-1), own_rows, sizes)

        pieces = 2 * (own_rows // sizes[0])

        def maker(r):
            def make(p, after):
                mine, other = sketch_pair(
                    scalars[pieces * p : pieces * (p + 1)], ids, child_block, samples[r], own_rows, sizes, after
                )
                other = lax.ppermute(other, "child", CORES)
                own = [mine[:, c : c + K // 2] + other[:, c : c + K // 2] for c in (0, K // 2)]
                return lax.optimization_barrier(own)

            return make

        def total(value):
            return group_sum(value, child_index)

        first_parts, steps = line_scatter(maker(0), {0: []})
        first_leaf = jnp.concatenate(first_parts, axis=1)
        second_parts, _ = line_scatter(maker(1), {0: steps[:1], 1: steps[1:]})
    else:
        places = lax.iota(jnp.int32, child_count * col_count)
        scalars = block_scalars(row_ids, leaf_base + places * own_rows, own_rows, sizes)

        pieces = own_rows // sizes[0]

        def leaf(r):
            blocks = []
            for p in range(0, child_count * col_count, 2):
                blocks += sketch_pair(scalars[p * pieces : (p + 2) * pieces], ids, child_block, samples[r], own_rows, sizes)
            return lax.psum_scatter(
                jnp.concatenate(blocks, axis=0), ("child", "col"), scatter_dimension=0, tiled=True
            )

        def total(value):
            return lax.psum(value, ("child", "col"))

        first_leaf = leaf(0)
        second_parts = [leaf(1)]

    gram = total(jnp.dot(first_leaf.T, first_leaf, precision=HI)) / leaf_rows
    inverse = inverse_factor(gram)
    leaf_basis = lax.dot_general(first_leaf, inverse, (((1,), (1,)), ((), ())), precision=HI)
    dual = jnp.dot(leaf_basis, inverse, precision=HI)
    fresh = []
    for second in second_parts:
        cross = total(jnp.dot(first_leaf.T, second, precision=HI)) / leaf_rows
        fresh.append(second - jnp.dot(dual, cross, precision=HI))
    return (leaf_basis, jnp.concatenate(fresh, axis=1))


def solution(mesh):
    placed = (P("child", "row", "col"), P(), P())
    return jax.shard_map(
        body,
        mesh=mesh,
        in_specs=placed,
        out_specs=(P(("row", "child", "col"), None), P(("row", "child", "col"), None)),
        check_vma=False,
    )
```

```python
import functools

import jax
import jax.numpy as jnp
import numpy as np
from jax import lax
from jax.experimental import pallas as pl
from jax.experimental.pallas import tpu as pltpu
from jax.sharding import PartitionSpec as P

NP = 24576
K = 256
HI = lax.Precision.HIGHEST
CORES = [(0, 1), (1, 0)]
MIB = 1024 * 1024
LIGHT = pl.CostEstimate(flops=0, bytes_accessed=0, transcendentals=0)


def sample_rows(seed_value, parents, sample_width):
    hashed = (
        parents[:, None] * 40503
        + lax.iota(jnp.int32, sample_width)[None, :] * 9973
        + seed_value * 2654435
    )
    hashed = hashed ^ hashed >> 15 & 131071
    hashed = hashed * 73244475
    hashed = hashed ^ hashed >> 13 & 524287
    hashed = hashed * 1274126177
    hashed = hashed ^ hashed >> 16 & 65535
    unit_value = (hashed & 16777215).astype(jnp.float32) * (1.0 / 16777216.0)
    return (unit_value - 0.5) * 3.4641016


DEPTH = 3


def row_chunk(rows):
    return rows // 8 if rows % 128 == 0 else rows


def tile_sizes(own_rows, block_rows):
    tile = max(d for d in range(8, min(own_rows, 240) + 1, 8) if own_rows % d == 0)
    return tile, min(256, block_rows)


def tile_scalars(row_ids, bases, own_rows):
    block_rows = row_ids.shape[0]
    tile, reach = tile_sizes(own_rows, block_rows)
    starts = bases[:, None] + lax.iota(jnp.int32, own_rows // tile)[None, :] * tile
    before = jnp.sum((row_ids[None, None, :] < starts[:, :, None]).astype(jnp.int32), axis=2)
    return jnp.concatenate([bases[:, None], jnp.minimum(before // 16 * 16, block_rows - reach)], axis=1)


def multiply(step, steps, first, schur_ref, samples_ref, held, sems):
    chunk = held.shape[1]

    def copy(s):
        slot = lax.rem(s, DEPTH)
        start = pl.multiple_of(first + s * chunk, 16)
        return pltpu.make_async_copy(schur_ref.at[pl.ds(start, chunk), :], held.at[slot], sems.at[slot])

    @pl.when(step == 0)
    def _():
        for s in range(min(DEPTH - 1, steps)):
            copy(s).start()

    @pl.when(step + DEPTH - 1 < steps)
    def _():
        copy(step + DEPTH - 1).start()

    copy(step).wait()
    value = jnp.dot(held[lax.rem(step, DEPTH)], samples_ref[...], preferred_element_type=jnp.float32)
    high = value.astype(jnp.bfloat16)
    return high, (value - high.astype(jnp.float32)).astype(jnp.bfloat16)


def spread(block, scal_ref, ids_ref, high_ref, low_ref, out_ref):
    tile, reach = tile_sizes(out_ref.shape[0], high_ref.shape[0])
    for i in range(out_ref.shape[0] // tile):
        child = pl.multiple_of(scal_ref[block, 1 + i], 16)
        lane = pl.multiple_of(child // 128 * 128, 128)
        ids = pltpu.roll(ids_ref[:, pl.ds(lane, 384)], lax.rem(384 - (child - lane), 384), 1)
        ids = jnp.broadcast_to(ids[0:1, :reach], (tile, reach))
        wanted = scal_ref[block, 0] + i * tile + lax.broadcasted_iota(jnp.int32, (tile, reach), 0)
        select = (ids == wanted).astype(jnp.float32).astype(jnp.bfloat16)
        out_ref[i * tile : (i + 1) * tile, :] = jnp.dot(
            select, high_ref[pl.ds(child, reach), :], preferred_element_type=jnp.float32
        ) + jnp.dot(select, low_ref[pl.ds(child, reach), :], preferred_element_type=jnp.float32)


def multiply_kernel(steps, schur_ref, samples_ref, high_ref, low_ref, held, sems):
    high_ref[...], low_ref[...] = multiply(pl.program_id(0), steps, 0, schur_ref, samples_ref, held, sems)


def sketch_kernel(steps, heads, scal_ref, ids_ref, schur_ref, samples_ref, *refs):
    head_refs = refs[:heads]
    mine_ref, first_ref, rest_ref, held, high, low, sems = refs[heads:]
    step = pl.program_id(0)
    chunk = held.shape[1]
    done = high.shape[0] - steps * chunk
    block = step - steps
    even = lax.rem(block, 2) == 0

    if heads:

        @pl.when(step == 0)
        def _():
            high[:done, :] = head_refs[0][...]
            low[:done, :] = head_refs[1][...]

    @pl.when(step < steps)
    def _():
        rows = pl.ds(pl.multiple_of(done + step * chunk, 16), chunk)
        high[rows, :], low[rows, :] = multiply(step, steps, done, schur_ref, samples_ref, held, sems)

    for chosen, out_ref in ((block == 0, first_ref), (even & (block > 0), rest_ref), (~even & (block > 0), mine_ref)):

        @pl.when(chosen)
        def _(out_ref=out_ref):
            spread(block, scal_ref, ids_ref, high, low, out_ref)


VMEM = pl.BlockSpec(memory_space=pltpu.VMEM)


def multiply_rows(child_block, samples, rows):
    block_rows, block_cols = child_block.shape
    width = samples.shape[1]
    chunk = row_chunk(block_rows)
    return pl.pallas_call(
        functools.partial(multiply_kernel, rows // chunk),
        out_shape=[jax.ShapeDtypeStruct((rows, width), jnp.bfloat16)] * 2,
        grid=(rows // chunk,),
        in_specs=[pl.BlockSpec(memory_space=pl.ANY), VMEM],
        out_specs=[pl.BlockSpec((chunk, width), lambda s: (s, 0))] * 2,
        scratch_shapes=[
            pltpu.VMEM((DEPTH, chunk, block_cols), jnp.bfloat16),
            pltpu.SemaphoreType.DMA((DEPTH,)),
        ],
        compiler_params=pltpu.CompilerParams(vmem_limit_bytes=24 * MIB),
        cost_estimate=LIGHT,
        name="multiply",
    )(child_block, samples)


def sketch(scalars, ids, child_block, samples, own_rows, heads=()):
    block_rows, block_cols = child_block.shape
    width = samples.shape[1]
    chunk = row_chunk(block_rows)
    steps = (block_rows - (heads[0].shape[0] if heads else 0)) // chunk
    pairs = scalars.shape[0] // 2

    def output(count, skipped):
        shape = jax.ShapeDtypeStruct((count * own_rows, width), jnp.float32)
        index = lambda s, _: (jnp.clip((s - steps) // 2 - skipped, 0, count - 1), 0)
        return shape, pl.BlockSpec((own_rows, width), index)

    shapes, specs = zip(output(pairs, 0), output(1, 0), output(pairs - 1, 1))
    return pl.pallas_call(
        functools.partial(sketch_kernel, steps, len(heads)),
        out_shape=shapes,
        grid_spec=pltpu.PrefetchScalarGridSpec(
            num_scalar_prefetch=1,
            grid=(steps + scalars.shape[0],),
            in_specs=[VMEM, pl.BlockSpec(memory_space=pl.ANY), VMEM] + [VMEM] * len(heads),
            out_specs=specs,
            scratch_shapes=[
                pltpu.VMEM((DEPTH, chunk, block_cols), jnp.bfloat16),
                pltpu.VMEM((block_rows, width), jnp.bfloat16),
                pltpu.VMEM((block_rows, width), jnp.bfloat16),
                pltpu.SemaphoreType.DMA((DEPTH,)),
            ],
        ),
        compiler_params=pltpu.CompilerParams(vmem_limit_bytes=32 * MIB),
        cost_estimate=LIGHT,
        name="sketch",
    )(scalars, ids, child_block, samples, *heads)


def eliminate(tiles, size):
    count = size // 8
    sub = lax.broadcasted_iota(jnp.int32, (8, size), 0)
    lane = lax.broadcasted_iota(jnp.int32, (8, size), 1)
    rows = list(tiles)
    inverse = [(lane == sub + 8 * t).astype(jnp.float32) for t in range(count)]

    def row(value, k):
        return jnp.broadcast_to(value[k : k + 1, :], (8, size))

    for t in range(count):
        columns = [
            [jnp.broadcast_to(rows[i][:, 8 * t + k : 8 * t + k + 1], (8, size)) for k in range(8)]
            for i in range(t, count)
        ]
        diagonal = jnp.ones((8, size), jnp.float32)
        for k in range(8):
            pivot = row(columns[0][k], k)
            scale = 1.0 / pivot
            diagonal = jnp.where(sub == k, pivot, diagonal)
            heads = [row(columns[0][l], k) * scale for l in range(k + 1, 8)]
            head_row = row(rows[t], k) * scale
            head_inv = row(inverse[t], k) * scale
            for i in range(t, count):
                factor = columns[i - t][k]
                if i == t:
                    factor = jnp.where(sub > k, factor, 0.0)
                for l in range(k + 1, 8):
                    columns[i - t][l] = columns[i - t][l] - factor * heads[l - k - 1]
                rows[i] = rows[i] - factor * head_row
                inverse[i] = inverse[i] - factor * head_inv
        inverse[t] = inverse[t] * lax.rsqrt(diagonal)
    return jnp.concatenate(inverse, axis=0)


def factor_kernel(gram_ref, out_ref):
    half = gram_ref.shape[0] // 2

    def dot(a, b, dims):
        return lax.dot_general(a, b, (dims, ((), ())), precision=HI, preferred_element_type=jnp.float32)

    first = eliminate([gram_ref[8 * t : 8 * t + 8, :half] for t in range(half // 8)], half)
    lower = dot(gram_ref[half:, :half], first, ((1,), (1,)))
    rest = gram_ref[half:, half:] - dot(lower, lower, ((1,), (1,)))
    second = eliminate([rest[8 * t : 8 * t + 8, :] for t in range(half // 8)], half)
    out_ref[:half, :half] = first
    out_ref[:half, half:] = jnp.zeros((half, half), jnp.float32)
    out_ref[half:, :half] = -dot(second, dot(lower, first, ((1,), (0,))), ((1,), (0,)))
    out_ref[half:, half:] = second


def inverse_factor(gram):
    return pl.pallas_call(
        factor_kernel,
        out_shape=jax.ShapeDtypeStruct(gram.shape, jnp.float32),
        compiler_params=pltpu.CompilerParams(vmem_limit_bytes=16 * MIB),
        cost_estimate=LIGHT,
        name="inverse_factor",
    )(gram)


ORDER = np.array([[3, 2, 1, 0], [3, 2, 0, 1], [0, 1, 3, 2], [0, 1, 2, 3]], np.int32)
INWARD = [(0, 1), (3, 2)]
ACROSS = [(1, 2), (2, 1)]
PAIRS = [(0, 1), (1, 0), (2, 3), (3, 2)]
CROSSED = [(0, 2), (2, 0), (1, 3), (3, 1)]


def hop(value, pairs):
    return lax.ppermute(value, "col", pairs)


def fence(*values):
    return lax.optimization_barrier(values)


def add_kernel(widths, *refs):
    refs = list(refs)
    outs = refs[sum(len(w) for w in widths[:-1]) :]
    terms = []
    for w in widths[:-1]:
        terms.append((refs[: len(w)], w))
        refs = refs[len(w) :]

    def columns(parts, low, high):
        start = 0
        for ref, width in zip(*parts):
            if start <= low and high <= start + width:
                return ref[:, low - start : high - start]
            start += width

    cuts = sorted({sum(w[:i]) for w in widths for i in range(len(w) + 1)})
    for low, high in zip(cuts, cuts[1:]):
        value = sum(columns(term, low, high) for term in terms)
        start = 0
        for ref, width in zip(outs, widths[-1]):
            if start <= low and high <= start + width:
                ref[:, low - start : high - start] = value
            start += width


def add(terms, parts, rows=None, places=None):
    rows = rows or terms[0][0].shape[0]
    places = places or [0] * len(terms)
    width = sum(part.shape[1] for part in terms[0])
    widths = [[part.shape[1] for part in term] for term in terms] + [[width // parts] * parts]
    specs = [
        pl.BlockSpec((rows, part.shape[1]), lambda s, place=place: (place, 0))
        for term, place in zip(terms, places)
        for part in term
    ]
    return pl.pallas_call(
        functools.partial(add_kernel, widths),
        out_shape=[jax.ShapeDtypeStruct((rows, width // parts), jnp.float32)] * parts,
        grid=(1,),
        in_specs=specs,
        out_specs=[pl.BlockSpec((rows, width // parts), lambda s: (0, 0))] * parts,
        compiler_params=pltpu.CompilerParams(vmem_limit_bytes=16 * MIB),
        cost_estimate=LIGHT,
        name="add",
    )(*[part for term in terms for part in term])


def plus(*terms):
    return add([[term] for term in terms], 1)[0]


def core_sum(value, child_index):
    half = value.shape[0] // 2
    mine = lax.dynamic_slice_in_dim(value, child_index * half, half)
    other = lax.dynamic_slice_in_dim(value, (1 - child_index) * half, half)
    return mine + lax.ppermute(other, "child", CORES)


def core_join(mine, child_index):
    other = lax.ppermute(mine, "child", CORES)
    low = jnp.where(child_index == 0, mine, other)
    high = jnp.where(child_index == 0, other, mine)
    return jnp.concatenate([low, high], axis=0)


def times_transposed(a, b):
    return lax.dot_general(a, b, (((1,), (1,)), ((), ())), precision=HI)


def body(schur_blocks, child_map, round_seeds):
    child_block = schur_blocks[0]
    block_rows, block_cols = child_block.shape
    child_count = lax.axis_size("child")
    col_count = lax.axis_size("col")
    row_count = lax.axis_size("row")
    child_index = lax.axis_index("child")
    row_index = lax.axis_index("row")
    col_index = lax.axis_index("col")
    own_map = lax.dynamic_index_in_dim(child_map, child_index, 0, keepdims=False)
    col_ids = lax.dynamic_slice_in_dim(own_map, col_index * block_cols, block_cols)
    row_ids = lax.dynamic_slice_in_dim(own_map, row_index * block_rows, block_rows)
    leaf_rows = NP // row_count
    own_rows = leaf_rows // (child_count * col_count)
    leaf_base = row_index * leaf_rows
    ids = jnp.broadcast_to(jnp.pad(row_ids, (0, 384), constant_values=-1)[None, :], (8, block_rows + 384))

    def sampled(r, ids):
        return sample_rows(round_seeds[r], ids, K).astype(jnp.bfloat16)

    if child_count == 2 and col_count == len(ORDER):
        places = lax.dynamic_index_in_dim(jnp.asarray(ORDER), col_index, 0, keepdims=False)
        turns = jnp.stack([1 - child_index, child_index])
        bases = leaf_base + (turns[None, :] * col_count + places[:, None]) * own_rows
        scalars = tile_scalars(row_ids, bases.reshape(-1), own_rows)

        def swap(value):
            return lax.ppermute(value, "child", CORES)

        def part(mine, rest, p):
            return add([[mine], [rest]], 1, own_rows, [p, p - 1])[0]

        mine, first, rest = sketch(scalars, ids, child_block, sampled(0, col_ids), own_rows)
        own0 = add([[mine], [swap(first)]], 2, own_rows)
        *own0, rest, late_ids = fence(*own0, rest, col_ids)

        in3 = [hop(half, INWARD) for half in own0]
        rest = swap(rest)
        samples, own1 = fence(sampled(1, late_ids), part(mine, rest, 1))
        in2 = hop(own1, INWARD)
        heads = multiply_rows(child_block, samples, block_rows // 4 * 3)
        own2, own3 = part(mine, rest, 2), part(mine, rest, 3)
        in3[0], own0[0], *heads = fence(in3[0], own0[0], *heads)
        mid1 = [hop(plus(own0[0], in3[0]), ACROSS)]
        in3[1], own0[1], *heads = fence(in3[1], own0[1], *heads)
        mid1 += [hop(plus(own0[1], in3[1]), ACROSS)]
        later = sketch(scalars, ids, child_block, samples, own_rows, heads)
        out1 = add([[own2], mid1], 1)[0]
        in2, out1, own1, own3, mine, first, rest = fence(in2, out1, own1, own3, *later)

        last = hop(out1, PAIRS)
        mid2 = hop(plus(own1, in2), ACROSS)
        own0 = list(add([[mine], [swap(first)]], 2, own_rows))
        in3 = [hop(half, INWARD) for half in own0]
        rest = swap(rest)
        own1, own2, own3_next = [part(mine, rest, p) for p in (1, 2, 3)]
        first_leaf = plus(plus(own3, last), mid2)
        first_leaf, own1, own2, own3 = fence(first_leaf, own1, own2, own3_next)
        in2 = hop(own1, INWARD)
        gram = lax.dot_general(first_leaf, first_leaf, (((0,), (0,)), ((), ())), precision=HI)
        gram = core_sum(gram, child_index)
        in3[0], own0[0], gram = fence(in3[0], own0[0], gram)
        mid1 = [hop(plus(own0[0], in3[0]), ACROSS)]
        in3[1], own0[1], gram = fence(in3[1], own0[1], gram)
        mid1 += [hop(plus(own0[1], in3[1]), ACROSS)]
        gram = gram + hop(gram, INWARD)
        out1 = add([[own2], mid1], 1)[0]
        in2, out1, own1, gram = fence(in2, out1, own1, gram)

        last = hop(out1, PAIRS)
        gram = gram + hop(gram, ACROSS)
        mid2 = hop(plus(own1, in2), ACROSS)
        second, gram = fence(plus(plus(own3, last), mid2), gram)
        cross = core_sum(jnp.dot(first_leaf.T, second, precision=HI), child_index)
        arrived = hop(jnp.concatenate([cross, gram], axis=0), PAIRS)
        cross = cross + arrived[: K // 2]
        edge = (col_index == 0) | (col_index == col_count - 1)
        gram = jnp.where(edge, arrived[K // 2 :], gram)
        cross = cross + hop(cross, CROSSED)
        inverse = inverse_factor(core_join(gram, child_index) / leaf_rows)
        leaf_basis = times_transposed(first_leaf, inverse)
        dual = jnp.dot(leaf_basis, inverse, precision=HI)
        cross, leaf_basis, dual = fence(cross, leaf_basis, dual)
        cross = core_join(cross, child_index) / leaf_rows
    else:
        bases = leaf_base + lax.iota(jnp.int32, child_count * col_count) * own_rows
        scalars = tile_scalars(row_ids, bases, own_rows)

        def leaf(r):
            odd, *even = sketch(scalars, ids, child_block, sampled(r, col_ids), own_rows)
            even = jnp.concatenate(even, axis=0)
            blocks = jnp.stack([even.reshape(-1, own_rows, K), odd.reshape(-1, own_rows, K)], axis=1)
            return lax.psum_scatter(
                blocks.reshape(leaf_rows, K), ("child", "col"), scatter_dimension=0, tiled=True
            )

        first_leaf = leaf(0)
        second = leaf(1)
        gram = lax.psum(jnp.dot(first_leaf.T, first_leaf, precision=HI), ("child", "col")) / leaf_rows
        inverse = inverse_factor(gram)
        cross = lax.psum(jnp.dot(first_leaf.T, second, precision=HI), ("child", "col")) / leaf_rows
        leaf_basis = times_transposed(first_leaf, inverse)
        dual = jnp.dot(leaf_basis, inverse, precision=HI)

    return (leaf_basis, second - jnp.dot(dual, cross, precision=HI))


def solution(mesh):
    placed = (P("child", "row", "col"), P(), P())
    return jax.shard_map(
        body,
        mesh=mesh,
        in_specs=placed,
        out_specs=(P(("row", "child", "col"), None), P(("row", "child", "col"), None)),
        check_vma=False,
    )
```

```python
import functools

import jax
import jax.numpy as jnp
import numpy as np
from jax import lax
from jax.experimental import pallas as pl
from jax.experimental.pallas import tpu as pltpu
from jax.sharding import PartitionSpec as P

NP = 24576
K = 256
HI = lax.Precision.HIGHEST
CORES = [(0, 1), (1, 0)]
MIB = 1024 * 1024
LIGHT = pl.CostEstimate(flops=0, bytes_accessed=0, transcendentals=0)


def sample_rows(seed_value, parents, sample_width):
    hashed = (
        parents[:, None] * 40503
        + lax.iota(jnp.int32, sample_width)[None, :] * 9973
        + seed_value * 2654435
    )
    hashed = hashed ^ hashed >> 15 & 131071
    hashed = hashed * 73244475
    hashed = hashed ^ hashed >> 13 & 524287
    hashed = hashed * 1274126177
    hashed = hashed ^ hashed >> 16 & 65535
    unit_value = (hashed & 16777215).astype(jnp.float32) * (1.0 / 16777216.0)
    return (unit_value - 0.5) * 3.4641016


DEPTH = 4


def row_chunk(rows):
    return rows // 8 if rows % 128 == 0 else rows


def tile_sizes(own_rows, block_rows):
    tile = max(d for d in range(8, min(own_rows, 240) + 1, 8) if own_rows % d == 0)
    return tile, min(256, block_rows)


def tile_scalars(row_ids, bases, own_rows):
    block_rows = row_ids.shape[0]
    tile, reach = tile_sizes(own_rows, block_rows)
    starts = bases[:, None] + lax.iota(jnp.int32, own_rows // tile)[None, :] * tile
    before = jnp.sum((row_ids[None, None, :] < starts[:, :, None]).astype(jnp.int32), axis=2)
    return jnp.concatenate([bases[:, None], jnp.minimum(before // 16 * 16, block_rows - reach)], axis=1)


def multiply(step, steps, first, schur_ref, samples_ref, held, sems):
    chunk = held.shape[1]

    def copy(s):
        slot = lax.rem(s, DEPTH)
        start = pl.multiple_of(first + s * chunk, 16)
        return pltpu.make_async_copy(schur_ref.at[pl.ds(start, chunk), :], held.at[slot], sems.at[slot])

    @pl.when(step == 0)
    def _():
        for s in range(min(DEPTH - 1, steps)):
            copy(s).start()

    @pl.when(step + DEPTH - 1 < steps)
    def _():
        copy(step + DEPTH - 1).start()

    copy(step).wait()
    value = jnp.dot(held[lax.rem(step, DEPTH)], samples_ref[...], preferred_element_type=jnp.float32)
    high = value.astype(jnp.bfloat16)
    return high, (value - high.astype(jnp.float32)).astype(jnp.bfloat16)


def spread(block, scal_ref, ids_ref, high_ref, low_ref, out_ref):
    tile, reach = tile_sizes(out_ref.shape[0], high_ref.shape[0])
    for i in range(out_ref.shape[0] // tile):
        child = pl.multiple_of(scal_ref[block, 1 + i], 16)
        lane = pl.multiple_of(jnp.minimum(child // 128 * 128, ids_ref.shape[1] - 384), 128)
        ids = pltpu.roll(ids_ref[:, pl.ds(lane, 384)], lax.rem(384 - (child - lane), 384), 1)
        ids = jnp.broadcast_to(ids[0:1, :reach], (tile, reach))
        wanted = scal_ref[block, 0] + i * tile + lax.broadcasted_iota(jnp.int32, (tile, reach), 0)
        select = (ids == wanted).astype(jnp.float32).astype(jnp.bfloat16)
        out_ref[i * tile : (i + 1) * tile, :] = jnp.dot(
            select, high_ref[pl.ds(child, reach), :], preferred_element_type=jnp.float32
        ) + jnp.dot(select, low_ref[pl.ds(child, reach), :], preferred_element_type=jnp.float32)


def multiply_kernel(steps, schur_ref, samples_ref, high_ref, low_ref, held, sems):
    high_ref[...], low_ref[...] = multiply(pl.program_id(0), steps, 0, schur_ref, samples_ref, held, sems)


def sketch_kernel(steps, heads, scal_ref, ids_ref, schur_ref, samples_ref, *refs):
    head_refs = refs[:heads]
    mine_ref, first_ref, rest_ref, held, high, low, sems = refs[heads:]
    step = pl.program_id(0)
    chunk = held.shape[1]
    done = high.shape[0] - steps * chunk
    place = step - steps

    if heads:

        @pl.when(step == 0)
        def _():
            high[:done, :] = head_refs[0][...]
            low[:done, :] = head_refs[1][...]

    @pl.when(step < steps)
    def _():
        rows = pl.ds(pl.multiple_of(done + step * chunk, 16), chunk)
        high[rows, :], low[rows, :] = multiply(step, steps, done, schur_ref, samples_ref, held, sems)

    for chosen, out_ref, block in (
        (place == 0, first_ref, 0),
        (place > 0, rest_ref, 2 * place),
        (place >= 0, mine_ref, 2 * place + 1),
    ):

        @pl.when(chosen)
        def _(out_ref=out_ref, block=block):
            spread(block, scal_ref, ids_ref, high, low, out_ref)


VMEM = pl.BlockSpec(memory_space=pltpu.VMEM)


def multiply_rows(child_block, samples, rows):
    block_rows, block_cols = child_block.shape
    width = samples.shape[1]
    chunk = row_chunk(block_rows)
    return pl.pallas_call(
        functools.partial(multiply_kernel, rows // chunk),
        out_shape=[jax.ShapeDtypeStruct((rows, width), jnp.bfloat16)] * 2,
        grid=(rows // chunk,),
        in_specs=[pl.BlockSpec(memory_space=pl.ANY), VMEM],
        out_specs=[pl.BlockSpec((chunk, width), lambda s: (s, 0))] * 2,
        scratch_shapes=[
            pltpu.VMEM((DEPTH, chunk, block_cols), jnp.bfloat16),
            pltpu.SemaphoreType.DMA((DEPTH,)),
        ],
        compiler_params=pltpu.CompilerParams(vmem_limit_bytes=32 * MIB),
        cost_estimate=LIGHT,
        name="multiply",
    )(child_block, samples)


def sketch(scalars, ids, child_block, samples, own_rows, heads=()):
    block_rows, block_cols = child_block.shape
    width = samples.shape[1]
    chunk = row_chunk(block_rows)
    steps = (block_rows - (heads[0].shape[0] if heads else 0)) // chunk
    pairs = scalars.shape[0] // 2

    def output(count, skipped):
        shape = jax.ShapeDtypeStruct((count * own_rows, width), jnp.float32)
        index = lambda s, _: (jnp.clip(s - steps - skipped, 0, count - 1), 0)
        return shape, pl.BlockSpec((own_rows, width), index)

    shapes, specs = zip(output(pairs, 0), output(1, 0), output(pairs - 1, 1))
    return pl.pallas_call(
        functools.partial(sketch_kernel, steps, len(heads)),
        out_shape=shapes,
        grid_spec=pltpu.PrefetchScalarGridSpec(
            num_scalar_prefetch=1,
            grid=(steps + pairs,),
            in_specs=[VMEM, pl.BlockSpec(memory_space=pl.ANY), VMEM] + [VMEM] * len(heads),
            out_specs=specs,
            scratch_shapes=[
                pltpu.VMEM((DEPTH, chunk, block_cols), jnp.bfloat16),
                pltpu.VMEM((block_rows, width), jnp.bfloat16),
                pltpu.VMEM((block_rows, width), jnp.bfloat16),
                pltpu.SemaphoreType.DMA((DEPTH,)),
            ],
        ),
        compiler_params=pltpu.CompilerParams(vmem_limit_bytes=40 * MIB),
        cost_estimate=LIGHT,
        name="sketch",
    )(scalars, ids, child_block, samples, *heads)


def eliminate(tiles, size):
    count = size // 8
    sub = lax.broadcasted_iota(jnp.int32, (8, size), 0)
    lane = lax.broadcasted_iota(jnp.int32, (8, size), 1)
    rows = list(tiles)
    inverse = [(lane == sub + 8 * t).astype(jnp.float32) for t in range(count)]

    def row(value, k):
        return jnp.broadcast_to(value[k : k + 1, :], (8, size))

    for t in range(count):
        columns = [
            [jnp.broadcast_to(rows[i][:, 8 * t + k : 8 * t + k + 1], (8, size)) for k in range(8)]
            for i in range(t, count)
        ]
        diagonal = jnp.ones((8, size), jnp.float32)
        for k in range(8):
            pivot = row(columns[0][k], k)
            scale = 1.0 / pivot
            diagonal = jnp.where(sub == k, pivot, diagonal)
            heads = [row(columns[0][l], k) * scale for l in range(k + 1, 8)]
            head_row = row(rows[t], k) * scale
            head_inv = row(inverse[t], k) * scale
            for i in range(t, count):
                factor = columns[i - t][k]
                if i == t:
                    factor = jnp.where(sub > k, factor, 0.0)
                for l in range(k + 1, 8):
                    columns[i - t][l] = columns[i - t][l] - factor * heads[l - k - 1]
                rows[i] = rows[i] - factor * head_row
                inverse[i] = inverse[i] - factor * head_inv
        inverse[t] = inverse[t] * lax.rsqrt(diagonal)
    return jnp.concatenate(inverse, axis=0)


def factor_kernel(gram_ref, out_ref):
    half = gram_ref.shape[0] // 2

    def dot(a, b, dims):
        return lax.dot_general(a, b, (dims, ((), ())), precision=HI, preferred_element_type=jnp.float32)

    first = eliminate([gram_ref[8 * t : 8 * t + 8, :half] for t in range(half // 8)], half)
    lower = dot(gram_ref[half:, :half], first, ((1,), (1,)))
    rest = gram_ref[half:, half:] - dot(lower, lower, ((1,), (1,)))
    second = eliminate([rest[8 * t : 8 * t + 8, :] for t in range(half // 8)], half)
    out_ref[:half, :half] = first
    out_ref[:half, half:] = jnp.zeros((half, half), jnp.float32)
    out_ref[half:, :half] = -dot(second, dot(lower, first, ((1,), (0,))), ((1,), (0,)))
    out_ref[half:, half:] = second


def inverse_factor(gram):
    return pl.pallas_call(
        factor_kernel,
        out_shape=jax.ShapeDtypeStruct(gram.shape, jnp.float32),
        compiler_params=pltpu.CompilerParams(vmem_limit_bytes=16 * MIB),
        cost_estimate=LIGHT,
        name="inverse_factor",
    )(gram)


ORDER = np.array([[3, 2, 1, 0], [3, 2, 0, 1], [0, 1, 3, 2], [0, 1, 2, 3]], np.int32)
INWARD = [(0, 1), (3, 2)]
ACROSS = [(1, 2), (2, 1)]
OUTWARD = [(1, 0), (2, 3)]
PAIRS = [(0, 1), (1, 0), (2, 3), (3, 2)]
CROSSED = [(0, 2), (2, 0), (1, 3), (3, 1)]


def hop(value, pairs):
    return lax.ppermute(value, "col", pairs)


def fence(*values):
    return lax.optimization_barrier(values)


def add_kernel(widths, *refs):
    refs = list(refs)
    outs = refs[sum(len(w) for w in widths[:-1]) :]
    terms = []
    for w in widths[:-1]:
        terms.append((refs[: len(w)], w))
        refs = refs[len(w) :]

    def columns(parts, low, high):
        start = 0
        for ref, width in zip(*parts):
            if start <= low and high <= start + width:
                return ref[:, low - start : high - start]
            start += width

    cuts = sorted({sum(w[:i]) for w in widths for i in range(len(w) + 1)})
    for low, high in zip(cuts, cuts[1:]):
        value = sum(columns(term, low, high) for term in terms)
        start = 0
        for ref, width in zip(outs, widths[-1]):
            if start <= low and high <= start + width:
                ref[:, low - start : high - start] = value
            start += width


def add(terms, parts, rows=None, places=None):
    rows = rows or terms[0][0].shape[0]
    places = places or [0] * len(terms)
    width = sum(part.shape[1] for part in terms[0])
    widths = [[part.shape[1] for part in term] for term in terms] + [[width // parts] * parts]
    specs = [
        pl.BlockSpec((rows, part.shape[1]), lambda s, place=place: (place, 0))
        for term, place in zip(terms, places)
        for part in term
    ]
    return pl.pallas_call(
        functools.partial(add_kernel, widths),
        out_shape=[jax.ShapeDtypeStruct((rows, width // parts), jnp.float32)] * parts,
        grid=(1,),
        in_specs=specs,
        out_specs=[pl.BlockSpec((rows, width // parts), lambda s: (0, 0))] * parts,
        compiler_params=pltpu.CompilerParams(vmem_limit_bytes=16 * MIB),
        cost_estimate=LIGHT,
        name="add",
    )(*[part for term in terms for part in term])


def plus(*terms):
    return add([[term] for term in terms], 1)[0]


def core_sum(value, child_index):
    half = value.shape[0] // 2
    mine = lax.dynamic_slice_in_dim(value, child_index * half, half)
    other = lax.dynamic_slice_in_dim(value, (1 - child_index) * half, half)
    return mine + lax.ppermute(other, "child", CORES)


def core_join(mine, child_index):
    other = lax.ppermute(mine, "child", CORES)
    low = jnp.where(child_index == 0, mine, other)
    high = jnp.where(child_index == 0, other, mine)
    return jnp.concatenate([low, high], axis=0)


def times_transposed(a, b):
    return lax.dot_general(a, b, (((1,), (1,)), ((), ())), precision=HI)


def body(schur_blocks, child_map, round_seeds):
    child_block = schur_blocks[0]
    block_rows, block_cols = child_block.shape
    child_count = lax.axis_size("child")
    col_count = lax.axis_size("col")
    row_count = lax.axis_size("row")
    child_index = lax.axis_index("child")
    row_index = lax.axis_index("row")
    col_index = lax.axis_index("col")
    col_ids = lax.dynamic_slice(child_map, (child_index, col_index * block_cols), (1, block_cols))[0]
    row_ids = lax.dynamic_slice(child_map, (child_index, row_index * block_rows), (1, block_rows))[0]
    leaf_rows = NP // row_count
    own_rows = leaf_rows // (child_count * col_count)
    leaf_base = row_index * leaf_rows
    ids = jnp.broadcast_to(row_ids[None, :], (8, block_rows))

    def sampled(r, ids):
        return sample_rows(round_seeds[r], ids, K).astype(jnp.bfloat16)

    if child_count == 2 and col_count == len(ORDER):
        places = lax.dynamic_index_in_dim(jnp.asarray(ORDER), col_index, 0, keepdims=False)
        turns = jnp.stack([1 - child_index, child_index])
        bases = leaf_base + (turns[None, :] * col_count + places[:, None]) * own_rows
        scalars = tile_scalars(row_ids, bases.reshape(-1), own_rows)

        def swap(value):
            return lax.ppermute(value, "child", CORES)

        def part(mine, rest, p):
            return add([[mine], [rest]], 1, own_rows, [p, p - 1])[0]

        mine, first, rest = sketch(scalars, ids, child_block, sampled(0, col_ids), own_rows)
        own0 = add([[mine], [swap(first)]], 2, own_rows)
        *own0, rest, late_ids = fence(*own0, rest, col_ids)

        in3 = [hop(half, INWARD) for half in own0]
        rest = swap(rest)
        samples, own1 = fence(sampled(1, late_ids), part(mine, rest, 1))
        in2 = hop(own1, INWARD)
        heads = multiply_rows(child_block, samples, block_rows // 4 * 3)
        own2, own3 = part(mine, rest, 2), part(mine, rest, 3)
        in3[0], own0[0], *heads = fence(in3[0], own0[0], *heads)
        mid1 = [hop(plus(own0[0], in3[0]), ACROSS)]
        in3[1], own0[1], *heads = fence(in3[1], own0[1], *heads)
        mid1 += [hop(plus(own0[1], in3[1]), ACROSS)]
        later = sketch(scalars, ids, child_block, samples, own_rows, heads)
        out1 = add([[own2], mid1], 1)[0]
        in2, out1, own1, own3, mine, first, rest = fence(in2, out1, own1, own3, *later)

        last = hop(out1, PAIRS)
        mid2 = hop(plus(own1, in2), ACROSS)
        own0 = list(add([[mine], [swap(first)]], 2, own_rows))
        in3 = [hop(half, INWARD) for half in own0]
        rest = swap(rest)
        own1, own2, own3_next = [part(mine, rest, p) for p in (1, 2, 3)]
        first_leaf = plus(plus(own3, last), mid2)
        first_leaf, own1, own2, own3 = fence(first_leaf, own1, own2, own3_next)
        in2 = hop(own1, INWARD)
        gram = lax.dot_general(first_leaf, first_leaf, (((0,), (0,)), ((), ())), precision=HI)
        gram = core_sum(gram, child_index)
        in3[0], own0[0], gram = fence(in3[0], own0[0], gram)
        mid1 = [hop(plus(own0[0], in3[0]), ACROSS)]
        in3[1], own0[1], gram = fence(in3[1], own0[1], gram)
        mid1 += [hop(plus(own0[1], in3[1]), ACROSS)]
        gram = gram + hop(gram, INWARD)
        out1 = add([[own2], mid1], 1)[0]
        in2, out1, own1, gram = fence(in2, out1, own1, gram)

        last = hop(out1, PAIRS)
        gram = gram + hop(gram, ACROSS)
        mid2 = hop(plus(own1, in2), ACROSS)
        second = plus(plus(own3, last), mid2)
        cross = core_sum(jnp.dot(first_leaf.T, second, precision=HI), child_index)
        edge = (col_index == 0) | (col_index == col_count - 1)
        gram = jnp.where(edge, hop(gram, OUTWARD), gram)
        cross = cross + hop(cross, PAIRS)
        cross, gram = fence(cross, gram)
        cross = cross + hop(cross, CROSSED)
        inverse = inverse_factor(core_join(gram, child_index) / leaf_rows)
        leaf_basis = times_transposed(first_leaf, inverse)
        dual = jnp.dot(leaf_basis, inverse, precision=HI)
        cross, leaf_basis, dual = fence(cross, leaf_basis, dual)
        cross = core_join(cross, child_index) / leaf_rows
    else:
        bases = leaf_base + lax.iota(jnp.int32, child_count * col_count) * own_rows
        scalars = tile_scalars(row_ids, bases, own_rows)

        def leaf(r):
            odd, *even = sketch(scalars, ids, child_block, sampled(r, col_ids), own_rows)
            even = jnp.concatenate(even, axis=0)
            blocks = jnp.stack([even.reshape(-1, own_rows, K), odd.reshape(-1, own_rows, K)], axis=1)
            return lax.psum_scatter(
                blocks.reshape(leaf_rows, K), ("child", "col"), scatter_dimension=0, tiled=True
            )

        first_leaf = leaf(0)
        second = leaf(1)
        gram = lax.psum(jnp.dot(first_leaf.T, first_leaf, precision=HI), ("child", "col")) / leaf_rows
        inverse = inverse_factor(gram)
        cross = lax.psum(jnp.dot(first_leaf.T, second, precision=HI), ("child", "col")) / leaf_rows
        leaf_basis = times_transposed(first_leaf, inverse)
        dual = jnp.dot(leaf_basis, inverse, precision=HI)

    return (leaf_basis, second - jnp.dot(dual, cross, precision=HI))


def solution(mesh):
    placed = (P("child", "row", "col"), P(), P())
    return jax.shard_map(
        body,
        mesh=mesh,
        in_specs=placed,
        out_specs=(P(("row", "child", "col"), None), P(("row", "child", "col"), None)),
        check_vma=False,
    )
```
